32 devices in a mesh: expert: 4 (over y, x), hidden: 8 (over z, core).
Axes of the slice: x: 2, y: 2, z: 4, core: 2. Of those that a mesh axis runs over, the one named last changes fastest.
Arguments:
- tokens: bfloat16 [192, 6144], P(('expert', 'hidden')), may hold values from -6 to 6
- routes: int32 [192, 2], P(('expert', 'hidden')), may hold values from 0 to 3, all different within a row; in each aligned block of 6 rows (0 to 5, 6 to 11, ...) at most 4 rows name the same one
- gate_probs: float32 [192, 2], P(('expert', 'hidden')), may hold values from 0.1 to 1
- cotangent: bfloat16 [192, 6144], P(('expert', 'hidden')), may hold values from -6 to 6
- w_gate: bfloat16 [4, 6144, 8192], P('expert', None, 'hidden'), may hold values from -0.078125 to 0.078125
- w_up: bfloat16 [4, 6144, 8192], P('expert', None, 'hidden'), may hold values from -0.078125 to 0.078125
- w_down: bfloat16 [4, 8192, 6144], P('expert', 'hidden'), may hold values from -0.0625 to 0.0625
Outputs:
- layer_out: bfloat16 [192, 6144], P(('expert', 'hidden'))
- grad_tokens: bfloat16 [192, 6144], P(('expert', 'hidden'))
- grad_gate: bfloat16 [4, 6144, 8192], P('expert', None, 'hidden')
- grad_up: bfloat16 [4, 6144, 8192], P('expert', None, 'hidden')
- grad_down: bfloat16 [4, 8192, 6144], P('expert', 'hidden')
The draws below stay inside these ranges and needn't reach their ends.
Inputs may be any that keep to these rules, and one draw needn't show every extreme that they name: `routes`: each row names two different experts. Within the tokens of one device (aligned blocks of 6 rows) no expert is named by more than 4 rows, a bound that some block reaches.
All inputs are finite; a program needn't handle non-finite values.
Results may differ from the reference program's by a relative error of at most 0.015.
Values may be sent and summed in bfloat16 or wider, within the bound.
A program may use at most 192 MiB of HBM per device.

```python
import math
import jax
import jax.numpy as jnp
import numpy as np
from jax import lax

D = 6144
FF = 8192
EXPERTS = 4
TOK_DEV = 6
CAP = 4
TOKENS = 192
FF_BLK = 1024


def level_of(rng, extent, cuts, least, top_value):
    level = 1.0
    for position, shards_of in cuts:
        draws = jax.random.uniform(jax.random.fold_in(jax.random.fold_in(rng, 6), position), (shards_of,), jnp.float32, least / len(cuts), top_value / len(cuts))
        level = level * jnp.repeat(jnp.exp(draws), extent[position] // shards_of).reshape((-1,) + (1,) * (len(extent) - 1 - position))
    return level


def shared_out(key, own, number, rows, count, top, bound, lean):
    order = jax.random.permutation(key, count)
    packed, usual = shares(count, rows * top, bound, lean, True), shares(count, rows * top, bound, lean, False)
    places = jnp.arange(count)

    def named(tallies, rotation):
        used = int((tallies > 0).sum())
        fixed = max(1, used // 4)
        moved = fixed + (places - fixed + rotation * (used - fixed)) % max(1, count - fixed)
        return jnp.zeros((count,), jnp.int32).at[order[jnp.where(places < fixed, places, moved)]].set(jnp.asarray(tallies, jnp.int32))

    tallies = jnp.where(number % 4 == 0, named(packed, number // 4), named(usual, number - number // 4 - 1))
    mixed = jax.random.permutation(jax.random.fold_in(own, 3), count)
    donor, receiver = mixed[0:count // 2 * 2:2], mixed[1:count // 2 * 2:2]
    slack = jnp.minimum(tallies[donor] - 1, bound - tallies[receiver]) // 2
    slack = jnp.where((donor == order[0]) | (receiver == order[0]) | (tallies[receiver] == 0), 0, jnp.maximum(slack, 0))
    moved = jax.random.randint(jax.random.fold_in(own, 4), (count // 2,), 0, 1 << 20) % (slack + 1)
    tallies = tallies.at[donor].add(-moved).at[receiver].add(moved)
    items = jnp.searchsorted(jnp.cumsum(tallies), jnp.arange(rows * top), side="right").astype(jnp.int32)
    grid = items.reshape(top, rows).T
    grid = grid[jax.random.permutation(jax.random.fold_in(own, 1), rows)]
    rotation = jax.random.randint(jax.random.fold_in(own, 2), (rows, 1), 0, top)
    return jnp.take_along_axis(grid, (jnp.arange(top)[None, :] + rotation) % top, axis=1)


def shares(amount, total, most, skew, full):
    loads = [(1 << 20) // math.isqrt(rank ** skew) + 1 for rank in range(1, amount + 1)]
    largest = most if full else min(most, max(-(-total // amount), total * loads[0] // sum(loads)))
    least = 1 if total - largest >= amount - 1 else 0
    counts, spare = [largest] + [least] * (amount - 1), total - largest - least * (amount - 1)
    while spare > 0:
        free = [i for i in range(1, amount) if counts[i] < largest] or [i for i in range(1, amount) if counts[i] < most]
        mass, remaining = sum([loads[i] for i in free]), spare
        for i in free:
            more = min(most - counts[i], max(1, remaining * loads[i] // mass), spare)
            counts[i] = counts[i] + more
            spare = spare - more
    return np.array(counts)


def centred(stream_key, dims, width, reach, pieces=(), held_as=jnp.bfloat16):
    drawn = jax.random.normal(stream_key, dims, jnp.float32) * width
    if len(pieces) > 0:
        drawn = level_of(stream_key, dims, pieces, -0.22, 0.18) * drawn
    return jnp.clip(drawn, min=-reach, max=reach).astype(held_as)


def setup_inputs(seed: int = 0) -> dict:
    splits = jax.random.split(jax.random.key(seed), 8)
    tokens = centred(splits[0], (TOKENS, D), 1.0, 6.0, ((0, 32),))
    routes_keys = jax.random.split(jax.random.fold_in(splits[1], 1), TOKENS // TOK_DEV)
    routes_turns = jax.random.permutation(jax.random.fold_in(splits[1], 3), TOKENS // TOK_DEV)
    routes = jax.vmap(lambda own, number: shared_out(jax.random.fold_in(splits[1], 2), own, number, TOK_DEV, EXPERTS, 2, CAP, 2))(routes_keys, routes_turns).reshape((TOKENS, 2))
    gate_probs = jnp.clip(0.1 + 0.9 * jax.random.uniform(splits[2], (TOKENS, 2), jnp.float32) ** level_of(splits[2], (TOKENS, 2), ((0, 32),), -0.2, 0.2), 0.1, 1.0)
    cotangent = centred(splits[3], (TOKENS, D), 1.0, 6.0, ((0, 32),))
    w_gate = centred(splits[4], (EXPERTS, D, FF), D ** -0.5, 0.078125, ((0, 4), (2, 8)))
    w_up = centred(splits[5], (EXPERTS, D, FF), D ** -0.5, 0.078125, ((0, 4), (2, 8)))
    w_down = centred(splits[6], (EXPERTS, FF, D), FF ** -0.5, 0.0625, ((0, 4), (1, 8)))
    return {"tokens": tokens, "routes": routes, "gate_probs": gate_probs, "cotangent": cotangent, "w_gate": w_gate, "w_up": w_up, "w_down": w_down}


def slot_table(route_ids, experts, capacity):
    flat_ids = route_ids.reshape(-1)
    hits = (flat_ids[:, None] == jnp.arange(experts, dtype=jnp.int32)[None, :]).astype(jnp.int32)
    before = jnp.cumsum(hits, axis=0) - hits
    ranks = jnp.sum(before * hits, axis=1).astype(jnp.int32)
    slot_ids = flat_ids * capacity + ranks
    table = (slot_ids[:, None] == jnp.arange(experts * capacity, dtype=jnp.int32)[None, :]).astype(jnp.float32)
    return table.reshape(route_ids.shape[0], 2, experts * capacity)


def dispatch_tables(route_ids, gate_probs, experts, capacity):
    table = slot_table(route_ids, experts, capacity)
    placed = jnp.sum(table, axis=1)
    weighted = jnp.sum(table * gate_probs[:, :, None], axis=1)
    return placed, weighted


def expert_pass(expert_rows, grad_rows, gate_w, up_w, down_w):
    pre_gate = jnp.dot(expert_rows, gate_w, preferred_element_type=jnp.float32)
    pre_up = jnp.dot(expert_rows, up_w, preferred_element_type=jnp.float32)
    sig_gate = jax.nn.sigmoid(pre_gate)
    hidden = (pre_gate * sig_gate * pre_up).astype(jnp.bfloat16)
    grad_hidden = jnp.dot(grad_rows, down_w.T, preferred_element_type=jnp.float32)
    grad_pre_gate = (grad_hidden * pre_up * sig_gate * (1.0 + pre_gate * (1.0 - sig_gate))).astype(jnp.bfloat16)
    grad_pre_up = (grad_hidden * pre_gate * sig_gate).astype(jnp.bfloat16)
    grad_down = jnp.dot(hidden.T, grad_rows, preferred_element_type=jnp.float32).astype(jnp.bfloat16)
    grad_gate = jnp.dot(expert_rows.T, grad_pre_gate, preferred_element_type=jnp.float32).astype(jnp.bfloat16)
    grad_up = jnp.dot(expert_rows.T, grad_pre_up, preferred_element_type=jnp.float32).astype(jnp.bfloat16)
    count = expert_rows.shape[0]
    nblocks = FF // FF_BLK
    hid_blocks = hidden.reshape(count, nblocks, FF_BLK).transpose(1, 0, 2)
    gpg_blocks = grad_pre_gate.reshape(count, nblocks, FF_BLK).transpose(1, 0, 2)
    gpu_blocks = grad_pre_up.reshape(count, nblocks, FF_BLK).transpose(1, 0, 2)
    down_blocks = down_w.reshape(nblocks, FF_BLK, D)
    gate_blocks = gate_w.reshape(D, nblocks, FF_BLK).transpose(1, 0, 2)
    up_blocks = up_w.reshape(D, nblocks, FF_BLK).transpose(1, 0, 2)

    def add_block(carry, item):
        hid_b, gpg_b, gpu_b, down_b, gate_b, up_b = item
        part_out = lax.optimization_barrier(jnp.dot(hid_b, down_b, preferred_element_type=jnp.float32).astype(jnp.bfloat16))
        part_back = jnp.dot(gpg_b, gate_b.T, preferred_element_type=jnp.float32) + jnp.dot(gpu_b, up_b.T, preferred_element_type=jnp.float32)
        part_back = lax.optimization_barrier(part_back.astype(jnp.bfloat16))
        return (carry[0] + part_out.astype(jnp.float32), carry[1] + part_back.astype(jnp.float32)), None

    zeros = jnp.zeros((count, D), jnp.float32)
    (out_sum, back_sum), unused = lax.scan(add_block, (zeros, zeros), (hid_blocks, gpg_blocks, gpu_blocks, down_blocks, gate_blocks, up_blocks))
    return out_sum.astype(jnp.bfloat16), back_sum.astype(jnp.bfloat16), grad_gate, grad_up, grad_down


def reference(tokens, routes, gate_probs, cotangent, w_gate, w_up, w_down):
    nblk = TOKENS // TOK_DEV
    tok_blocks = tokens.reshape(nblk, TOK_DEV, D)
    cot_blocks = cotangent.reshape(nblk, TOK_DEV, D)
    route_blocks = routes.reshape(nblk, TOK_DEV, 2)
    prob_blocks = gate_probs.reshape(nblk, TOK_DEV, 2)
    placed, weighted = jax.vmap(lambda ids, probs: dispatch_tables(ids, probs, EXPERTS, CAP))(route_blocks, prob_blocks)
    sent_in = jnp.einsum('btc,btd->bcd', placed, tok_blocks.astype(jnp.float32), precision=lax.Precision.HIGHEST).astype(jnp.bfloat16)
    sent_grad = jnp.einsum('btc,btd->bcd', weighted, cot_blocks.astype(jnp.float32), precision=lax.Precision.HIGHEST).astype(jnp.bfloat16)
    expert_in = sent_in.reshape(nblk, EXPERTS, CAP, D).transpose(1, 0, 2, 3).reshape(EXPERTS, nblk * CAP, D)
    expert_grad = sent_grad.reshape(nblk, EXPERTS, CAP, D).transpose(1, 0, 2, 3).reshape(EXPERTS, nblk * CAP, D)
    outs_e, backs_e, grad_gate, grad_up, grad_down = lax.map(lambda item: expert_pass(*item), (expert_in, expert_grad, w_gate, w_up, w_down))
    outs_b = outs_e.reshape(EXPERTS, nblk, CAP, D).transpose(1, 0, 2, 3).reshape(nblk, EXPERTS * CAP, D)
    backs_b = backs_e.reshape(EXPERTS, nblk, CAP, D).transpose(1, 0, 2, 3).reshape(nblk, EXPERTS * CAP, D)
    layer_out = jnp.einsum('btc,bcd->btd', weighted, outs_b.astype(jnp.float32), precision=lax.Precision.HIGHEST).astype(jnp.bfloat16)
    grad_tokens = jnp.einsum('btc,bcd->btd', placed, backs_b.astype(jnp.float32), precision=lax.Precision.HIGHEST).astype(jnp.bfloat16)
    return layer_out.reshape(TOKENS, D), grad_tokens.reshape(TOKENS, D), grad_gate, grad_up, grad_down
```

```python
import functools

import jax
import jax.numpy as jnp
from jax import lax
from jax.experimental import pallas as pl
from jax.experimental.pallas import tpu as pltpu
from jax.sharding import PartitionSpec as P

CHUNKS = 4
META = 128
MESH = pl.DeviceIdType.MESH


def gather_kernel(experts, hidden, blk_ref, out_ref, send_sem, recv_sem):
    e = lax.axis_index("expert")
    h = lax.axis_index("hidden")
    chips = hidden // 2
    chip, core = h // 2, h % 2
    x, y = e % 2, e // 2
    step_x, step_y = 1 - 2 * x, 2 - 4 * y
    near = e + (1 - core) * step_x + core * step_y
    far = e + core * step_x + (1 - core) * step_y
    diag = e + step_x + step_y
    sibling = h + 1 - 2 * core

    def slot(ee, c):
        return (c * 2 + core) * experts + ee

    def copy(kind, ident, dev, own=False):
        return pltpu.make_async_remote_copy(
            src_ref=blk_ref if own else out_ref.at[ident],
            dst_ref=out_ref.at[ident],
            send_sem=send_sem.at[kind, ident],
            recv_sem=recv_sem.at[ident],
            device_id=dev,
            device_id_type=MESH,
        )

    up, down = (e, h + 2), (e, h - 2)
    to_near, to_far, to_sib = (near, h), (far, h), (e, sibling)
    has_up, has_down = chip < chips - 1, chip > 0

    barrier = pltpu.get_barrier_semaphore()
    for dev in (to_near, to_far, to_sib):
        pl.semaphore_signal(barrier, inc=1, device_id=dev, device_id_type=MESH)

    @pl.when(has_up)
    def _():
        pl.semaphore_signal(barrier, inc=1, device_id=up, device_id_type=MESH)

    @pl.when(has_down)
    def _():
        pl.semaphore_signal(barrier, inc=1, device_id=down, device_id_type=MESH)

    pl.semaphore_wait(barrier, 3 + has_up.astype(jnp.int32) + has_down.astype(jnp.int32))

    def publish(ident, own=False):
        copy(2, ident, to_near, own).start()
        copy(3, ident, to_far, own).start()
        copy(4, ident, to_sib, own).start()

    def plane(c):
        a, b, d = slot(near, c), slot(far, c), slot(diag, c)
        copy(0, a, to_near).wait_recv()
        copy(3, a, to_far).start()
        copy(4, a, to_sib).start()
        copy(0, b, to_far).wait_recv()
        copy(4, b, to_sib).start()
        copy(0, d, to_near).wait_recv()
        copy(4, d, to_sib).start()

    mine = slot(e, chip)

    @pl.when(has_up)
    def _():
        copy(0, mine, up, True).start()

    @pl.when(has_down)
    def _():
        copy(1, mine, down, True).start()

    publish(mine, True)
    out_ref[pl.ds(mine, 1)] = blk_ref[...][None]

    for k in range(1, chips):

        @pl.when(chip >= k)
        def _():
            ident = slot(e, chip - k)
            copy(0, ident, up).wait_recv()

            @pl.when(has_up)
            def _():
                copy(0, ident, up).start()

            publish(ident)

        @pl.when(chip + k < chips)
        def _():
            ident = slot(e, chip + k)
            copy(1, ident, down).wait_recv()

            @pl.when(has_down)
            def _():
                copy(1, ident, down).start()

            publish(ident)

        if k == 1:
            plane(chip)
        else:

            @pl.when(chip >= k - 1)
            def _():
                plane(chip - (k - 1))

            @pl.when(chip + (k - 1) < chips)
            def _():
                plane(chip + (k - 1))

    if chips == 1:
        plane(chip)
    else:

        @pl.when(chip >= chips - 1)
        def _():
            plane(chip - (chips - 1))

        @pl.when(chip + (chips - 1) < chips)
        def _():
            plane(chip + (chips - 1))

    for c in range(chips):
        for ee in range(experts):
            ident = (c * 2 + 1 - core) * experts + ee
            copy(4, ident, to_sib).wait_recv()
    for c in range(chips):
        ident = slot(e, c)

        @pl.when(has_up & (chip >= c))
        def _():
            copy(0, ident, up).wait_send()

        @pl.when(has_down & (chip <= c))
        def _():
            copy(1, ident, down).wait_send()

        copy(2, ident, to_near).wait_send()
        copy(3, ident, to_far).wait_send()
        copy(3, slot(near, c), to_far).wait_send()
        for ee in range(experts):
            copy(4, slot(ee, c), to_sib).wait_send()


def gather_blocks(block, experts, hidden):
    count = experts * hidden
    return pl.pallas_call(
        functools.partial(gather_kernel, experts, hidden),
        out_shape=jax.ShapeDtypeStruct((count,) + block.shape, block.dtype),
        in_specs=[pl.BlockSpec(memory_space=pltpu.VMEM)],
        out_specs=pl.BlockSpec(memory_space=pltpu.VMEM),
        scratch_shapes=[
            pltpu.SemaphoreType.DMA((5, count)),
            pltpu.SemaphoreType.DMA((count,)),
        ],
        compiler_params=pltpu.CompilerParams(
            collective_id=0, has_side_effects=True, vmem_limit_bytes=48 * 1024 * 1024
        ),
    )(block)


def place_kernel(rows, width, pick_ref, scale_ref, all_ref, in_ref, grad_ref):
    got = jnp.dot(pick_ref[0, 0], all_ref[:, :width], preferred_element_type=jnp.float32)
    in_ref[...] = got[:rows].astype(jnp.bfloat16)
    grad_ref[...] = (got[rows:] * scale_ref[...]).astype(jnp.bfloat16)


def dispatch(tokens, routes, gate_probs, cotangent, experts, hidden, capacity):
    count, width = tokens.shape
    part = width // CHUNKS
    rows2 = 2 * count
    both = jnp.concatenate([tokens, cotangent], axis=0)
    body = both.reshape(rows2, CHUNKS, part).transpose(1, 0, 2)
    high = lax.reduce_precision(gate_probs, 8, 7)
    rest = gate_probs - high
    middle = lax.reduce_precision(rest, 8, 7)
    low = rest - middle
    meta = jnp.concatenate(
        [routes.astype(jnp.float32), high, middle, low], axis=1
    ).astype(jnp.bfloat16)
    meta = jnp.pad(meta, ((0, rows2 - count), (0, META - 8)))
    meta = jnp.broadcast_to(meta[None], (CHUNKS, rows2, META))
    block = jnp.concatenate([body, meta], axis=2).reshape(CHUNKS * rows2, part + META)
    gathered = gather_blocks(block, experts, hidden)
    blocks = experts * hidden
    meta = gathered[:, :count, part : part + 8].astype(jnp.float32)
    ids = meta[:, :, :2]
    probs = meta[:, :, 2:4] + meta[:, :, 4:6] + meta[:, :, 6:8]
    here = lax.axis_index("expert").astype(jnp.float32)
    hits = (ids.reshape(blocks, 2 * count) == here).astype(jnp.int32)
    order = jnp.tril(jnp.ones((2 * count, 2 * count), jnp.int32), -1)
    ranks = jnp.sum(hits[:, None, :] * order[None], axis=2)
    pick = (hits[:, None, :] == 1) & (
        ranks[:, None, :] == jnp.arange(capacity, dtype=jnp.int32)[None, :, None]
    )
    pick = pick.astype(jnp.float32).reshape(blocks, capacity, count, 2)
    scale = jnp.sum(pick * probs[:, None], axis=(2, 3)).reshape(blocks * capacity, 1)
    pick = jnp.sum(pick, axis=3).reshape(blocks * capacity, count)
    size = 16 if blocks % 16 == 0 else blocks
    groups, rows = blocks // size, size * capacity
    width_all = size * CHUNKS * rows2
    col = jnp.arange(width_all, dtype=jnp.int32)
    col_tok = col % count
    col_kind = (col // count) % 2
    col_chunk = (col // rows2) % CHUNKS
    col_block = col // (rows2 * CHUNKS)
    spread = (col_tok[None, :] == jnp.arange(count, dtype=jnp.int32)[:, None]).astype(jnp.bfloat16)
    tiled = jnp.dot(pick.astype(jnp.bfloat16), spread, preferred_element_type=jnp.float32)
    tiled = tiled.reshape(groups, rows, width_all)
    own = col_block[None, :] == (jnp.arange(rows, dtype=jnp.int32) // capacity)[:, None]
    tiled = jnp.where(own[None], tiled, 0.0).astype(jnp.bfloat16)
    chunk_ok = col_chunk[None, :] == jnp.arange(CHUNKS, dtype=jnp.int32)[:, None]
    kind_ok = col_kind[None, :] == jnp.arange(2, dtype=jnp.int32)[:, None]
    keep = (chunk_ok[:, None, :] & kind_ok[None]).astype(jnp.bfloat16)
    pick_all = keep[None, :, :, None, :] * tiled[:, None, None]
    pick_all = pick_all.reshape(groups, CHUNKS, 2 * rows, width_all)
    flat = gathered.reshape(groups * width_all, part + META)
    shape = jax.ShapeDtypeStruct((groups * rows, width), jnp.bfloat16)
    return pl.pallas_call(
        functools.partial(place_kernel, rows, part),
        grid=(groups, CHUNKS),
        out_shape=(shape, shape),
        in_specs=[
            pl.BlockSpec((1, 1, 2 * rows, width_all), lambda g, c: (g, c, 0, 0)),
            pl.BlockSpec((rows, 1), lambda g, c: (g, 0)),
            pl.BlockSpec((width_all, part + META), lambda g, c: (g, 0)),
        ],
        out_specs=(
            pl.BlockSpec((rows, part), lambda g, c: (g, c)),
            pl.BlockSpec((rows, part), lambda g, c: (g, c)),
        ),
        compiler_params=pltpu.CompilerParams(vmem_limit_bytes=40 * 1024 * 1024),
    )(pick_all, scale, flat)


def slot_table(route_ids, experts, capacity):
    flat_ids = route_ids.reshape(-1)
    hits = (flat_ids[:, None] == jnp.arange(experts, dtype=jnp.int32)[None, :]).astype(jnp.int32)
    pairs = flat_ids.shape[0]
    earlier = jnp.tril(jnp.ones((pairs, pairs), jnp.int32), -1)
    before = jnp.sum(earlier[:, :, None] * hits[None], axis=1)
    ranks = jnp.sum(before * hits, axis=1)
    slot_ids = flat_ids * capacity + ranks
    table = (slot_ids[:, None] == jnp.arange(experts * capacity, dtype=jnp.int32)[None, :]).astype(
        jnp.float32
    )
    return table.reshape(route_ids.shape[0], 2, experts * capacity)


def on_device(tokens, routes, gate_probs, cotangent, w_gate, w_up, w_down):
    experts = lax.axis_size("expert")
    width = tokens.shape[1]
    capacity = (2 * tokens.shape[0] + experts - 1) // experts + 1
    table = slot_table(routes, experts, capacity)
    placed = jnp.sum(table, axis=1)
    weighted = jnp.sum(table * gate_probs[:, :, None], axis=1)
    expert_rows, grad_rows = dispatch(
        tokens, routes, gate_probs, cotangent, experts, lax.axis_size("hidden"), capacity
    )
    gate_w = w_gate[0]
    up_w = w_up[0]
    down_w = w_down[0]
    pre_gate = jnp.dot(expert_rows, gate_w, preferred_element_type=jnp.float32)
    pre_up = jnp.dot(expert_rows, up_w, preferred_element_type=jnp.float32)
    sig_gate = jax.nn.sigmoid(pre_gate)
    hidden = (pre_gate * sig_gate * pre_up).astype(jnp.bfloat16)
    summed_out = lax.psum_scatter(
        jnp.dot(hidden, down_w, preferred_element_type=jnp.float32).astype(jnp.bfloat16),
        "hidden",
        scatter_dimension=0,
        tiled=True,
    )
    expert_out = summed_out.reshape(experts, capacity, width)
    returned = lax.all_to_all(expert_out, "expert", split_axis=0, concat_axis=0, tiled=True)
    layer_out = jnp.dot(
        weighted, returned.reshape(-1, width).astype(jnp.float32), precision=lax.Precision.HIGHEST
    ).astype(jnp.bfloat16)
    grad_hidden = jnp.dot(grad_rows, down_w.T, preferred_element_type=jnp.float32)
    grad_pre_gate = (grad_hidden * pre_up * sig_gate * (1.0 + pre_gate * (1.0 - sig_gate))).astype(
        jnp.bfloat16
    )
    grad_pre_up = (grad_hidden * pre_gate * sig_gate).astype(jnp.bfloat16)
    grad_down = jnp.dot(hidden.T, grad_rows, preferred_element_type=jnp.float32).astype(
        jnp.bfloat16
    )
    grad_gate = jnp.dot(expert_rows.T, grad_pre_gate, preferred_element_type=jnp.float32).astype(
        jnp.bfloat16
    )
    grad_up = jnp.dot(expert_rows.T, grad_pre_up, preferred_element_type=jnp.float32).astype(
        jnp.bfloat16
    )
    first = jnp.dot(grad_pre_gate, gate_w.T, preferred_element_type=jnp.float32)
    summed_back = lax.psum_scatter(
        (first + jnp.dot(grad_pre_up, up_w.T, preferred_element_type=jnp.float32)).astype(
            jnp.bfloat16
        ),
        "hidden",
        scatter_dimension=0,
        tiled=True,
    )
    expert_back = summed_back.reshape(experts, capacity, width)
    returned_back = lax.all_to_all(expert_back, "expert", split_axis=0, concat_axis=0, tiled=True)
    grad_tokens = jnp.dot(
        placed,
        returned_back.reshape(-1, width).astype(jnp.float32),
        precision=lax.Precision.HIGHEST,
    ).astype(jnp.bfloat16)
    return (layer_out, grad_tokens, grad_gate[None], grad_up[None], grad_down[None])


def solution(mesh):
    return jax.shard_map(
        on_device,
        mesh=mesh,
        in_specs=(
            P(("expert", "hidden"), None),
            P(("expert", "hidden"), None),
            P(("expert", "hidden"), None),
            P(("expert", "hidden"), None),
            P("expert", None, "hidden"),
            P("expert", None, "hidden"),
            P("expert", "hidden", None),
        ),
        out_specs=(
            P(("expert", "hidden"), None),
            P(("expert", "hidden"), None),
            P("expert", None, "hidden"),
            P("expert", None, "hidden"),
            P("expert", "hidden", None),
        ),
        check_vma=False,
    )
```

```python
import functools

import jax
import jax.numpy as jnp
from jax import lax
from jax.experimental import pallas as pl
from jax.experimental.pallas import tpu as pltpu
from jax.sharding import PartitionSpec as P

CHUNKS = 4
META = 128
MESH = pl.DeviceIdType.MESH


def gather_kernel(experts, hidden, blk_ref, out_ref, send_sem, recv_sem):
    e = lax.axis_index("expert")
    h = lax.axis_index("hidden")
    chips = hidden // 2
    chip, core = h // 2, h % 2
    x, y = e % 2, e // 2
    step_x, step_y = 1 - 2 * x, 2 - 4 * y
    near = e + (1 - core) * step_x + core * step_y
    far = e + core * step_x + (1 - core) * step_y
    diag = e + step_x + step_y
    sibling = h + 1 - 2 * core

    def slot(ee, c):
        return (c * 2 + core) * experts + ee

    def copy(kind, ident, dev, own=False):
        return pltpu.make_async_remote_copy(
            src_ref=blk_ref if own else out_ref.at[ident],
            dst_ref=out_ref.at[ident],
            send_sem=send_sem.at[kind, ident],
            recv_sem=recv_sem.at[ident],
            device_id=dev,
            device_id_type=MESH,
        )

    up, down = (e, h + 2), (e, h - 2)
    to_near, to_far, to_sib = (near, h), (far, h), (e, sibling)
    has_up, has_down = chip < chips - 1, chip > 0

    barrier = pltpu.get_barrier_semaphore()
    for dev in (to_near, to_far, to_sib):
        pl.semaphore_signal(barrier, inc=1, device_id=dev, device_id_type=MESH)

    @pl.when(has_up)
    def _():
        pl.semaphore_signal(barrier, inc=1, device_id=up, device_id_type=MESH)

    @pl.when(has_down)
    def _():
        pl.semaphore_signal(barrier, inc=1, device_id=down, device_id_type=MESH)

    pl.semaphore_wait(barrier, 3 + has_up.astype(jnp.int32) + has_down.astype(jnp.int32))

    def publish(ident, own=False):
        copy(2, ident, to_near, own).start()
        copy(3, ident, to_far, own).start()
        copy(4, ident, to_sib, own).start()

    def plane(c):
        a, b, d = slot(near, c), slot(far, c), slot(diag, c)
        copy(0, a, to_near).wait_recv()
        copy(3, a, to_far).start()
        copy(4, a, to_sib).start()
        copy(0, b, to_far).wait_recv()
        copy(4, b, to_sib).start()
        copy(0, d, to_near).wait_recv()
        copy(4, d, to_sib).start()

    mine = slot(e, chip)

    @pl.when(has_up)
    def _():
        copy(0, mine, up, True).start()

    @pl.when(has_down)
    def _():
        copy(1, mine, down, True).start()

    publish(mine, True)
    out_ref[pl.ds(mine, 1)] = blk_ref[...][None]

    for k in range(1, chips):

        @pl.when(chip >= k)
        def _():
            ident = slot(e, chip - k)
            copy(0, ident, up).wait_recv()

            @pl.when(has_up)
            def _():
                copy(0, ident, up).start()

            publish(ident)

        @pl.when(chip + k < chips)
        def _():
            ident = slot(e, chip + k)
            copy(1, ident, down).wait_recv()

            @pl.when(has_down)
            def _():
                copy(1, ident, down).start()

            publish(ident)

        if k == 1:
            plane(chip)
        else:

            @pl.when(chip >= k - 1)
            def _():
                plane(chip - (k - 1))

            @pl.when(chip + (k - 1) < chips)
            def _():
                plane(chip + (k - 1))

    if chips == 1:
        plane(chip)
    else:

        @pl.when(chip >= chips - 1)
        def _():
            plane(chip - (chips - 1))

        @pl.when(chip + (chips - 1) < chips)
        def _():
            plane(chip + (chips - 1))

    for c in range(chips):
        for ee in range(experts):
            ident = (c * 2 + 1 - core) * experts + ee
            copy(4, ident, to_sib).wait_recv()
    for c in range(chips):
        ident = slot(e, c)

        @pl.when(has_up & (chip >= c))
        def _():
            copy(0, ident, up).wait_send()

        @pl.when(has_down & (chip <= c))
        def _():
            copy(1, ident, down).wait_send()

        copy(2, ident, to_near).wait_send()
        copy(3, ident, to_far).wait_send()
        copy(3, slot(near, c), to_far).wait_send()
        for ee in range(experts):
            copy(4, slot(ee, c), to_sib).wait_send()


def gather_blocks(block, experts, hidden):
    count = experts * hidden
    return pl.pallas_call(
        functools.partial(gather_kernel, experts, hidden),
        out_shape=jax.ShapeDtypeStruct((count,) + block.shape, block.dtype),
        in_specs=[pl.BlockSpec(memory_space=pltpu.VMEM)],
        out_specs=pl.BlockSpec(memory_space=pltpu.VMEM),
        scratch_shapes=[
            pltpu.SemaphoreType.DMA((5, count)),
            pltpu.SemaphoreType.DMA((count,)),
        ],
        compiler_params=pltpu.CompilerParams(
            collective_id=0, has_side_effects=True, vmem_limit_bytes=48 * 1024 * 1024
        ),
    )(block)


def place_kernel(rows, width, pick_ref, scale_ref, all_ref, in_ref, grad_ref):
    got = jnp.dot(pick_ref[0, 0], all_ref[:, :width], preferred_element_type=jnp.float32)
    in_ref[...] = got[:rows].astype(jnp.bfloat16)
    grad_ref[...] = (got[rows:] * scale_ref[...]).astype(jnp.bfloat16)


def dispatch(tokens, routes, gate_probs, cotangent, experts, hidden, capacity):
    count, width = tokens.shape
    part = width // CHUNKS
    rows2 = 2 * count
    both = jnp.concatenate([tokens, cotangent], axis=0)
    body = both.reshape(rows2, CHUNKS, part).transpose(1, 0, 2)
    high = lax.reduce_precision(gate_probs, 8, 7)
    rest = gate_probs - high
    middle = lax.reduce_precision(rest, 8, 7)
    low = rest - middle
    meta = jnp.concatenate(
        [routes.astype(jnp.float32), high, middle, low], axis=1
    ).astype(jnp.bfloat16)
    meta = jnp.pad(meta, ((0, rows2 - count), (0, META - 8)))
    meta = jnp.broadcast_to(meta[None], (CHUNKS, rows2, META))
    block = jnp.concatenate([body, meta], axis=2).reshape(CHUNKS * rows2, part + META)
    gathered = gather_blocks(block, experts, hidden)
    blocks = experts * hidden
    meta = gathered[:, :count, part : part + 8].astype(jnp.float32)
    ids = meta[:, :, :2]
    probs = meta[:, :, 2:4] + meta[:, :, 4:6] + meta[:, :, 6:8]
    here = lax.axis_index("expert").astype(jnp.float32)
    hits = (ids.reshape(blocks, 2 * count) == here).astype(jnp.int32)
    order = jnp.tril(jnp.ones((2 * count, 2 * count), jnp.int32), -1)
    ranks = jnp.sum(hits[:, None, :] * order[None], axis=2)
    pick = (hits[:, None, :] == 1) & (
        ranks[:, None, :] == jnp.arange(capacity, dtype=jnp.int32)[None, :, None]
    )
    pick = pick.astype(jnp.float32).reshape(blocks, capacity, count, 2)
    scale = jnp.sum(pick * probs[:, None], axis=(2, 3)).reshape(blocks * capacity, 1)
    pick = jnp.sum(pick, axis=3).reshape(blocks * capacity, count)
    size = 16 if blocks % 16 == 0 else blocks
    groups, rows = blocks // size, size * capacity
    width_all = size * CHUNKS * rows2
    col = jnp.arange(width_all, dtype=jnp.int32)
    col_tok = col % count
    col_kind = (col // count) % 2
    col_chunk = (col // rows2) % CHUNKS
    col_block = col // (rows2 * CHUNKS)
    spread = (col_tok[None, :] == jnp.arange(count, dtype=jnp.int32)[:, None]).astype(jnp.bfloat16)
    tiled = jnp.dot(pick.astype(jnp.bfloat16), spread, preferred_element_type=jnp.float32)
    tiled = tiled.reshape(groups, rows, width_all)
    own = col_block[None, :] == (jnp.arange(rows, dtype=jnp.int32) // capacity)[:, None]
    tiled = jnp.where(own[None], tiled, 0.0).astype(jnp.bfloat16)
    chunk_ok = col_chunk[None, :] == jnp.arange(CHUNKS, dtype=jnp.int32)[:, None]
    kind_ok = col_kind[None, :] == jnp.arange(2, dtype=jnp.int32)[:, None]
    keep = (chunk_ok[:, None, :] & kind_ok[None]).astype(jnp.bfloat16)
    pick_all = keep[None, :, :, None, :] * tiled[:, None, None]
    pick_all = pick_all.reshape(groups, CHUNKS, 2 * rows, width_all)
    flat = gathered.reshape(groups * width_all, part + META)
    shape = jax.ShapeDtypeStruct((groups * rows, width), jnp.bfloat16)
    return pl.pallas_call(
        functools.partial(place_kernel, rows, part),
        grid=(groups, CHUNKS),
        out_shape=(shape, shape),
        in_specs=[
            pl.BlockSpec((1, 1, 2 * rows, width_all), lambda g, c: (g, c, 0, 0)),
            pl.BlockSpec((rows, 1), lambda g, c: (g, 0)),
            pl.BlockSpec((width_all, part + META), lambda g, c: (g, 0)),
        ],
        out_specs=(
            pl.BlockSpec((rows, part), lambda g, c: (g, c)),
            pl.BlockSpec((rows, part), lambda g, c: (g, c)),
        ),
        compiler_params=pltpu.CompilerParams(vmem_limit_bytes=40 * 1024 * 1024),
    )(pick_all, scale, flat)


def hidden_kernel(x_ref, g_ref, gate_ref, up_ref, down_ref, h_ref, da_ref, du_ref):
    pre = jnp.dot(x_ref[...], gate_ref[0], preferred_element_type=jnp.float32)
    up = jnp.dot(x_ref[...], up_ref[0], preferred_element_type=jnp.float32)
    grad = lax.dot_general(
        g_ref[...],
        down_ref[0],
        (((1,), (1,)), ((), ())),
        preferred_element_type=jnp.float32,
    )
    sig = jax.nn.sigmoid(pre)
    h_ref[...] = (pre * sig * up).astype(jnp.bfloat16)
    da_ref[...] = (grad * up * sig * (1.0 + pre * (1.0 - sig))).astype(jnp.bfloat16)
    du_ref[...] = (grad * pre * sig).astype(jnp.bfloat16)


def hidden_grads(expert_rows, grad_rows, w_gate, w_up, w_down):
    rows, width = expert_rows.shape
    units = w_gate.shape[2]
    tile = 256 if units % 256 == 0 else units
    shape = jax.ShapeDtypeStruct((rows, units), jnp.bfloat16)
    part = pl.BlockSpec((rows, tile), lambda i: (0, i))
    whole = pl.BlockSpec((rows, width), lambda i: (0, 0), pipeline_mode=pl.Buffered(1))
    return pl.pallas_call(
        hidden_kernel,
        grid=(units // tile,),
        out_shape=(shape, shape, shape),
        in_specs=[
            whole,
            whole,
            pl.BlockSpec((1, width, tile), lambda i: (0, 0, i)),
            pl.BlockSpec((1, width, tile), lambda i: (0, 0, i)),
            pl.BlockSpec((1, tile, width), lambda i: (0, i, 0)),
        ],
        out_specs=(part, part, part),
        compiler_params=pltpu.CompilerParams(vmem_limit_bytes=44 * 1024 * 1024),
        cost_estimate=pl.CostEstimate(
            flops=6 * rows * width * units,
            bytes_accessed=6 * width * units,
            transcendentals=rows * units,
        ),
    )(expert_rows, grad_rows, w_gate, w_up, w_down)


def slot_table(route_ids, experts, capacity):
    flat_ids = route_ids.reshape(-1)
    hits = (flat_ids[:, None] == jnp.arange(experts, dtype=jnp.int32)[None, :]).astype(jnp.int32)
    pairs = flat_ids.shape[0]
    earlier = jnp.tril(jnp.ones((pairs, pairs), jnp.int32), -1)
    before = jnp.sum(earlier[:, :, None] * hits[None], axis=1)
    ranks = jnp.sum(before * hits, axis=1)
    slot_ids = flat_ids * capacity + ranks
    table = (slot_ids[:, None] == jnp.arange(experts * capacity, dtype=jnp.int32)[None, :]).astype(
        jnp.float32
    )
    return table.reshape(route_ids.shape[0], 2, experts * capacity)


def on_device(tokens, routes, gate_probs, cotangent, w_gate, w_up, w_down):
    experts = lax.axis_size("expert")
    width = tokens.shape[1]
    capacity = (2 * tokens.shape[0] + experts - 1) // experts + 1
    table = slot_table(routes, experts, capacity)
    placed = jnp.sum(table, axis=1)
    weighted = jnp.sum(table * gate_probs[:, :, None], axis=1)
    expert_rows, grad_rows = dispatch(
        tokens, routes, gate_probs, cotangent, experts, lax.axis_size("hidden"), capacity
    )
    gate_w = w_gate[0]
    up_w = w_up[0]
    down_w = w_down[0]
    hidden, grad_pre_gate, grad_pre_up = hidden_grads(
        expert_rows, grad_rows, w_gate, w_up, w_down
    )
    summed_out = lax.psum_scatter(
        jnp.dot(hidden, down_w, preferred_element_type=jnp.float32).astype(jnp.bfloat16),
        "hidden",
        scatter_dimension=0,
        tiled=True,
    )
    expert_out = summed_out.reshape(experts, capacity, width)
    returned = lax.all_to_all(expert_out, "expert", split_axis=0, concat_axis=0, tiled=True)
    layer_out = jnp.dot(
        weighted, returned.reshape(-1, width).astype(jnp.float32), precision=lax.Precision.HIGHEST
    ).astype(jnp.bfloat16)
    grad_down = jnp.dot(hidden.T, grad_rows, preferred_element_type=jnp.float32).astype(
        jnp.bfloat16
    )
    grad_gate = jnp.dot(expert_rows.T, grad_pre_gate, preferred_element_type=jnp.float32).astype(
        jnp.bfloat16
    )
    grad_up = jnp.dot(expert_rows.T, grad_pre_up, preferred_element_type=jnp.float32).astype(
        jnp.bfloat16
    )
    first = jnp.dot(grad_pre_gate, gate_w.T, preferred_element_type=jnp.float32)
    summed_back = lax.psum_scatter(
        (first + jnp.dot(grad_pre_up, up_w.T, preferred_element_type=jnp.float32)).astype(
            jnp.bfloat16
        ),
        "hidden",
        scatter_dimension=0,
        tiled=True,
    )
    expert_back = summed_back.reshape(experts, capacity, width)
    returned_back = lax.all_to_all(expert_back, "expert", split_axis=0, concat_axis=0, tiled=True)
    grad_tokens = jnp.dot(
        placed,
        returned_back.reshape(-1, width).astype(jnp.float32),
        precision=lax.Precision.HIGHEST,
    ).astype(jnp.bfloat16)
    return (layer_out, grad_tokens, grad_gate[None], grad_up[None], grad_down[None])


def solution(mesh):
    return jax.shard_map(
        on_device,
        mesh=mesh,
        in_specs=(
            P(("expert", "hidden"), None),
            P(("expert", "hidden"), None),
            P(("expert", "hidden"), None),
            P(("expert", "hidden"), None),
            P("expert", None, "hidden"),
            P("expert", None, "hidden"),
            P("expert", "hidden", None),
        ),
        out_specs=(
            P(("expert", "hidden"), None),
            P(("expert", "hidden"), None),
            P("expert", None, "hidden"),
            P("expert", None, "hidden"),
            P("expert", "hidden", None),
        ),
        check_vma=False,
    )
```
